32 devices in a mesh: sta: 8 (over y, x, core), win: 4 (over z).
Axes of the slice: x: 2, y: 2, z: 4, core: 2. Of those that a mesh axis runs over, the one named last changes fastest.
Arguments:
- traces: float32 [64, 64, 2048], P('sta', 'win'), may hold values from -24 to 24
- gap_mask: int32 [64, 64], P('sta', 'win'), may hold values 0 or 1
- pair_mask: int32 [64, 5, 8], P('sta'), may hold values from 0 to 1, as said below
Outputs:
- pws: float32 [64, 5, 8, 512], P('sta', None, None, 'win')
The draws below stay inside these ranges and needn't reach their ends.
Inputs may be any that keep to these rules, and one draw needn't show every extreme that they name: pair_mask is 0 for a station paired with itself (offset index 2, same station of the block).
All inputs are finite; a program needn't handle non-finite values. No bound on the sum of `gap_mask` on one device may be relied on, other than what follows from the above.
Results may differ from the reference program's by a relative error of at most 0.0003.
Values may be sent and summed in bfloat16 or wider, within the bound.
No kernel may reach another device: no remote copies, remote signals or barrier semaphores. Data moves between devices by JAX's collectives and lax.ppermute only.
A program may use at most 128 MiB of HBM per device.

```python
import math
import jax
import jax.numpy as jnp
from jax import lax

SB = 8
SAMPLES = 2048
F = 1024
LAGS = 512
WBLK = 128
REACH = 2
STATIONS = 64
WINDOWS = 64
N_STA = 8


def draw_traces(key, part):
    source_key = jax.random.fold_in(key, 101)
    delay_key = jax.random.fold_in(key, 202)
    sign_key = jax.random.fold_in(key, 303)
    noise_key = jax.random.fold_in(key, 404)
    strength_key = jax.random.fold_in(key, 505)
    source = jnp.clip(jax.random.normal(source_key, (WINDOWS, SAMPLES), jnp.float32), -6.0, 6.0)
    delays = jax.random.randint(delay_key, (STATIONS,), 0, LAGS // 4).astype(jnp.int32)
    polarity = jax.random.randint(sign_key, (STATIONS,), 0, 2).astype(jnp.float32) * 2.0 - 1.0
    noise = jnp.clip(jax.random.normal(noise_key, (STATIONS, WINDOWS, SAMPLES), jnp.float32), -6.0, 6.0)
    strength = jnp.exp(jax.random.uniform(strength_key, (STATIONS,), jnp.float32, 0.0, math.log(3.0)))
    positions = (jnp.arange(SAMPLES, dtype=jnp.int32)[None, :] - delays[:, None]) % SAMPLES
    moved = jnp.take(source, positions, axis=1)
    coherent = jnp.transpose(moved, (1, 0, 2))
    return ((strength * polarity)[:, None, None] * coherent + noise).astype(jnp.float32)


def draw_pair_mask(key, part):
    choose_key = jax.random.fold_in(key, 606)
    kept = (jax.random.randint(choose_key, (STATIONS, 2 * REACH + 1, SB), 0, 5) < 4).astype(jnp.int32)
    station = jnp.arange(STATIONS, dtype=jnp.int32) % SB
    offset = jnp.arange(2 * REACH + 1, dtype=jnp.int32)
    partner = jnp.arange(SB, dtype=jnp.int32)
    itself = (station[:, None, None] == partner[None, None, :]) & (offset[None, :, None] == REACH)
    return jnp.where(itself, 0, kept).astype(jnp.int32)


def plant(array, own_key, smallest, high):
    extent = array.shape
    index_at = [jax.random.randint(jax.random.fold_in(own_key, axis), (), 0, extent[axis]) for axis in range(len(extent))]
    array = array.at[tuple(index_at)].set(smallest)
    longest = extent.index(max(extent))
    index_at[longest] = (index_at[longest] + 1) % extent[longest]
    return array.at[tuple(index_at)].set(high)


def setup_inputs(seed: int = 0) -> dict:
    seeds = jax.random.split(jax.random.key(seed), 4)
    return {
        "traces": draw_traces(jax.random.fold_in(seeds[3], 71), 0),
        "gap_mask": plant((jax.random.randint(seeds[1], (STATIONS, WINDOWS), 0, 4) < 3).astype(jnp.int32), jax.random.fold_in(seeds[1], 1), 0, 1),
        "pair_mask": draw_pair_mask(jax.random.fold_in(seeds[3], 71), 0),
    }


def transform_table():
    moments = jnp.arange(SAMPLES, dtype=jnp.int32)
    frequency = jnp.arange(F, dtype=jnp.int32)
    product = moments[:, None] * frequency[None, :] % SAMPLES
    angle = product.astype(jnp.float32) * (2.0 * math.pi / SAMPLES)
    return jnp.concatenate([jnp.cos(angle), -jnp.sin(angle)], axis=1)

def inverse_table():
    frequency = jnp.arange(F, dtype=jnp.int32)
    delays = jnp.arange(LAGS, dtype=jnp.int32) - LAGS // 2
    product = frequency[:, None] * delays[None, :] % SAMPLES
    angle = product.astype(jnp.float32) * (2.0 * math.pi / SAMPLES)
    cosine = jnp.cos(angle)
    sine = jnp.sin(angle)
    upper = jnp.concatenate([cosine, sine], axis=1)
    lower = jnp.concatenate([-sine, cosine], axis=1)
    return (jnp.concatenate([upper, lower], axis=0) * (1.0 / math.sqrt(F))).astype(jnp.bfloat16)

def whiten(traces):
    signs = jnp.sign(traces.astype(jnp.float32))
    flat = signs.reshape(-1, SAMPLES)
    spectra = jnp.dot(flat, transform_table(), precision=lax.Precision.HIGHEST, preferred_element_type=jnp.float32)
    real_part = spectra[:, :F]
    imag_part = spectra[:, F:]
    power = real_part * real_part + imag_part * imag_part
    bands = lax.optimization_barrier(jnp.mean(power.reshape(-1, F // WBLK, WBLK), axis=2))
    factor = 1.0 / jnp.sqrt(bands + 1e-05)
    factor = jnp.repeat(factor, WBLK, axis=1)
    white = jnp.concatenate([real_part * factor, imag_part * factor], axis=1).astype(jnp.bfloat16)
    return white.reshape(traces.shape[0], traces.shape[1], 2 * F)

def pair_terms(own_spectra, own_flags, far_spectra, far_flags, table):
    bin_count = own_spectra.shape[-1] // 2
    own_real = own_spectra[..., :bin_count].astype(jnp.float32)[:, None]
    own_imag = own_spectra[..., bin_count:].astype(jnp.float32)[:, None]
    far_real = far_spectra[..., :bin_count].astype(jnp.float32)[None]
    far_imag = far_spectra[..., bin_count:].astype(jnp.float32)[None]
    cross_real = own_real * far_real + own_imag * far_imag
    cross_imag = own_imag * far_real - own_real * far_imag
    cross = jnp.concatenate([cross_real, cross_imag], axis=-1).astype(jnp.bfloat16)
    lead = cross.shape[:3]
    analytic = jnp.dot(cross.reshape(-1, 2 * bin_count), table, preferred_element_type=jnp.float32)
    lag_count = table.shape[1] // 2
    analytic = analytic.reshape(lead + (2 * lag_count,))
    real_part = analytic[..., :lag_count]
    imag_part = analytic[..., lag_count:]
    magnitude = jnp.sqrt(real_part * real_part + imag_part * imag_part)
    divisor = jnp.maximum(magnitude, 0.5)
    weights = own_flags[:, None, :] * far_flags[None, :, :]
    linear = lax.optimization_barrier(jnp.sum(weights[..., None] * real_part, axis=2))
    phase_real = lax.optimization_barrier(jnp.sum(weights[..., None] * (real_part / divisor), axis=2))
    phase_imag = lax.optimization_barrier(jnp.sum(weights[..., None] * (imag_part / divisor), axis=2))
    counts = lax.optimization_barrier(jnp.sum(weights, axis=2))
    return (linear, phase_real, phase_imag, counts)

def reference(traces, gap_mask, pair_mask):
    white = whiten(traces)
    flags = gap_mask.astype(jnp.float32)
    table = inverse_table()
    blocks = white.reshape(N_STA, SB, white.shape[1], 2 * F)
    flag_blocks = flags.reshape(N_STA, SB, flags.shape[1])
    gathered = []
    for offset in range(2 * REACH + 1):
        moved = offset - REACH
        far_blocks = jnp.roll(blocks, -moved, axis=0)
        far_flags = jnp.roll(flag_blocks, -moved, axis=0)
        terms = lax.map(lambda items: pair_terms(items[0], items[1], items[2], items[3], table), (blocks, flag_blocks, far_blocks, far_flags))
        gathered.append(terms)
    linear = jnp.stack([item[0] for item in gathered], axis=2).reshape(N_STA * SB, 2 * REACH + 1, SB, LAGS)
    phase_real = jnp.stack([item[1] for item in gathered], axis=2).reshape(N_STA * SB, 2 * REACH + 1, SB, LAGS)
    phase_imag = jnp.stack([item[2] for item in gathered], axis=2).reshape(N_STA * SB, 2 * REACH + 1, SB, LAGS)
    counts = jnp.stack([item[3] for item in gathered], axis=2).reshape(N_STA * SB, 2 * REACH + 1, SB)
    divisor = jnp.maximum(counts, 1.0)[..., None]
    phase_real = phase_real / divisor
    phase_imag = phase_imag / divisor
    return linear / divisor * (phase_real * phase_real + phase_imag * phase_imag) * pair_mask.astype(jnp.float32)[..., None]
```

```python
import functools
import math

import jax
import jax.numpy as jnp
import ml_dtypes
import numpy as np
from jax import lax
from jax.experimental import pallas as pl
from jax.experimental.pallas import tpu as pltpu
from jax.sharding import PartitionSpec as P

SAMPLES = 2048
F = 1024
LAGS = 512
WBLK = 128
REACH = 2
LANES = 128
SLICES = F // LANES
HALF = LAGS // 2
PEAK = 34.0
EXTRA = 16
STACK = 4


def bins():
    m = np.arange(LANES // 2)
    rows = [np.concatenate([16 * m, 8 + 16 * m])]
    for s in range(1, SLICES):
        rows.append(np.concatenate([s + 16 * m, 16 - s + 16 * m]))
    return np.stack(rows)


def split(table):
    high = table.astype(ml_dtypes.bfloat16)
    low = (table - high.astype(np.float64)).astype(ml_dtypes.bfloat16)
    return high, low


def forward_tables():
    at = bins()
    t = np.arange(LANES)
    upper = (np.arange(LANES) >= LANES // 2)[None, :]
    tables = []
    for s in range(SLICES):
        angle = 2.0 * np.pi * ((t[:, None] * at[s][None, :]) % SAMPLES) / SAMPLES
        c, n = np.cos(angle), np.sin(angle)
        if s == 0:
            first = np.concatenate([np.where(upper, 0.0, c), np.where(upper, 0.0, -n)], axis=1)
            second = np.concatenate([np.where(upper, c, 0.0), np.where(upper, -n, 0.0)], axis=1)
        else:
            first = np.concatenate([c, -n], axis=1)
            second = np.concatenate([np.where(upper, -n, n), np.where(upper, -c, c)], axis=1)
        tables.append(np.concatenate([first, second], axis=0))
    return split(np.stack(tables))


def band_table():
    band = (np.arange(LANES) % (LANES // 2)) // (WBLK // 16)
    return (band[:, None] == band[None, :]).astype(np.float32)


def inverse_table():
    at = bins().reshape(-1)
    tau = np.arange(HALF)
    angle = (((at[:, None] * tau[None, :]) % SAMPLES).astype(np.float32)) * np.float32(2.0 * math.pi / SAMPLES)
    both = np.concatenate([np.cos(angle), np.sin(angle)], axis=1).astype(np.float32)
    return (both * np.float32(1.0 / math.sqrt(F))).astype(ml_dtypes.bfloat16)


def edge_table():
    scale = 1.0 / math.sqrt(F)
    sign = np.where(np.arange(LANES) < LANES // 2, 1.0, -1.0) * scale
    table = np.zeros((4 * LANES, 2 * LANES))
    cr, sr, ci, si = (slice(k * LANES, (k + 1) * LANES) for k in range(4))
    table[cr, 0], table[si, 0] = scale, -sign
    table[cr, 1], table[si, 1] = scale, sign
    table[sr, LANES], table[ci, LANES] = sign, scale
    table[sr, LANES + 1], table[ci, LANES + 1] = -sign, scale
    return table.astype(ml_dtypes.bfloat16)


ROOT = float(np.float32(ml_dtypes.bfloat16(math.sqrt(0.5))))


def stage_one(x):
    r = math.sqrt(0.5)
    a = [x[s] + x[s + 8] for s in range(8)]
    b = [x[s] - x[s + 8] for s in range(8)]
    c = [a[s] + a[s + 4] for s in range(4)]
    d = [a[s] - a[s + 4] for s in range(4)]
    e0, e1, g0, g1 = c[0] + c[2], c[1] + c[3], c[0] - c[2], c[1] - c[3]
    pairs = [None] * 8
    pairs[0] = (e0 + e1, e0 - e1)
    pairs[4] = (g0, -g1)
    near, far = r * (d[1] - d[3]), r * (d[1] + d[3])
    pairs[2] = (d[0] + near, -(d[2] + far))
    pairs[6] = (d[0] - near, d[2] - far)
    u = [None] + [b[s] - b[8 - s] for s in (1, 2, 3)]
    v = [None] + [b[s] + b[8 - s] for s in (1, 2, 3)]
    for k in (1, 3, 5, 7):
        real = b[0]
        imag = b[4] * math.sin(math.pi * k / 2)
        for s in (1, 2, 3):
            real = real + u[s] * math.cos(math.pi * s * k / 8)
            imag = imag + v[s] * math.sin(math.pi * s * k / 8)
        pairs[k] = (real, -imag)
    return pairs


def forward_kernel(stations, windows, traces, gaps, high, low, band, out, first, second):
    rows = stations * windows
    block = 16
    for start in range(0, rows, block):
        x = traces[start:start + block, :]
        x = jnp.where(x > 0, 1.0, jnp.where(x < 0, -1.0, 0.0))
        y = stage_one([x[:, s * LANES:(s + 1) * LANES] for s in range(16)])
        for s in range(SLICES):
            both = jnp.concatenate(y[s], axis=1)
            top = both.astype(jnp.bfloat16)
            first[s, start:start + block, :] = top
            second[s, start:start + block, :] = (both - top.astype(jnp.float32)).astype(jnp.bfloat16)
    spectra = []
    power = jnp.zeros((rows, LANES), jnp.float32)
    for s in range(SLICES):
        z = jnp.dot(first[s], high[s], preferred_element_type=jnp.float32)
        z += jnp.dot(second[s], high[s], preferred_element_type=jnp.float32)
        z += jnp.dot(first[s], low[s], preferred_element_type=jnp.float32)
        spectra.append(z)
        power += z[:, :LANES] * z[:, :LANES] + z[:, LANES:] * z[:, LANES:]
    bands = jnp.dot(power, band[...], precision=lax.Precision.HIGHEST, preferred_element_type=jnp.float32)
    factor = lax.rsqrt(bands * (1.0 / WBLK) + 1e-05)
    flags = gaps[...].astype(jnp.float32)
    keep = jnp.concatenate(
        [jnp.broadcast_to(flags[:, w:w + 1], (stations, LANES)) for w in range(windows)], axis=0
    )
    corner = lax.broadcasted_iota(jnp.int32, (rows, LANES), 1) == 0
    to = lax.broadcasted_iota(jnp.int32, (rows, rows), 0)
    source = lax.broadcasted_iota(jnp.int32, (rows, rows), 1)
    moved = (to // stations == source % windows) & (to % stations == source // windows)
    moved = jnp.where(moved, 1.0, 0.0).astype(jnp.bfloat16)
    factor = jnp.concatenate([factor, factor], axis=1)
    keep = jnp.concatenate([keep, keep], axis=1)
    for s in range(SLICES):
        white = (spectra[s] * factor).astype(jnp.bfloat16)
        white = jnp.dot(moved, white, preferred_element_type=jnp.float32) * keep
        real, imag = white[:, :LANES], white[:, LANES:]
        if s == 0:
            imag = jnp.where(corner, keep[:, :LANES], imag)
        out[:, s * LANES:(s + 1) * LANES] = real.astype(jnp.bfloat16)
        out[:, F + s * LANES:F + (s + 1) * LANES] = imag.astype(jnp.bfloat16)


def forward(traces, gaps):
    stations, windows, samples = traces.shape
    rows = stations * windows
    high, low = forward_tables()
    return pl.pallas_call(
        functools.partial(forward_kernel, stations, windows),
        out_shape=jax.ShapeDtypeStruct((rows, 2 * F), jnp.bfloat16),
        scratch_shapes=[pltpu.VMEM((SLICES, rows, 2 * LANES), jnp.bfloat16)] * 2,
        compiler_params=pltpu.CompilerParams(vmem_limit_bytes=40 * 1024 * 1024),
        cost_estimate=pl.CostEstimate(flops=6 * rows * F * 512, bytes_accessed=4 << 20, transcendentals=rows * LANES),
        name="whiten",
    )(traces.reshape(rows, samples), gaps, jnp.asarray(high), jnp.asarray(low), jnp.asarray(band_table()))


def unit_kernel(stations, windows, parts, choose, *refs):
    x_ref, refs = refs[0], refs[1:]
    y_refs, refs = refs[:2 if choose else 1], refs[2 if choose else 1:]
    table, edge = refs[:2]
    outs = refs[2:2 + parts]
    xf, yf, x0, y0, cross, fold, total, edges, counts = refs[2 + parts:]
    pairs = stations * stations
    rows = stations * windows
    me = lax.axis_index("win")

    def load(source, target, corner):
        lane = lax.broadcasted_iota(jnp.int32, (rows, LANES), 1) == 0
        for s in range(2 * SLICES):
            at = slice(s * LANES, (s + 1) * LANES)
            value = source[:, at].astype(jnp.float32)
            if s == SLICES:
                corner[...] = value.reshape(corner.shape)
                value = jnp.where(lane, 0.0, value)
            target[:, :, at] = value.reshape(windows, stations, LANES)

    load(x_ref, xf, x0)
    if choose:
        odd = lax.rem(lax.axis_index("sta"), 2)

        @pl.when(odd == 0)
        def _():
            load(y_refs[0], yf, y0)

        @pl.when(odd == 1)
        def _():
            load(y_refs[1], yf, y0)
    else:
        load(y_refs[0], yf, y0)

    total[...] = jnp.zeros_like(total)
    edges[...] = jnp.zeros_like(edges)
    counts[...] = jnp.zeros_like(counts)

    def step(chunk, carry):
        for v in range(STACK):
            w = chunk * STACK + v
            for i in range(0, stations, 2):
                folded = [[], [], [], []]
                for e in range(2):
                    at = pl.ds((i + e) * stations, stations)
                    counts[at, :] += x0[w, i + e:i + e + 1, :] * y0[w]
                place = pl.ds(v * pairs + i * stations, 2 * stations)
                reals, imags = [], []
                for s in range(SLICES):
                    re = slice(s * LANES, (s + 1) * LANES)
                    im = slice(F + s * LANES, F + (s + 1) * LANES)
                    yr, yi = yf[w, :, re], yf[w, :, im]
                    halves = []
                    for e in range(2):
                        xr, xi = xf[w, i + e:i + e + 1, re], xf[w, i + e:i + e + 1, im]
                        halves.append((xr * yr + xi * yi, xi * yr - xr * yi))
                    cr = jnp.concatenate([h[0] for h in halves], axis=0)
                    ci = jnp.concatenate([h[1] for h in halves], axis=0)
                    reals.append(cr)
                    imags.append(ci)
                    cross[0, place, re] = cr.astype(jnp.bfloat16)
                    cross[1, place, re] = ci.astype(jnp.bfloat16)
                for k, c in enumerate((reals, imags)):
                    cosine = (c[0] - c[4]) + ROOT * ((c[1] + c[7]) - (c[3] + c[5]))
                    sine = (c[2] - c[6]) + ROOT * ((c[1] + c[3]) - (c[5] + c[7]))
                    fold[place, 2 * k * LANES:(2 * k + 1) * LANES] = cosine.astype(jnp.bfloat16)
                    fold[place, (2 * k + 1) * LANES:(2 * k + 2) * LANES] = sine.astype(jnp.bfloat16)
        from_real = jnp.dot(cross[0], table[...], preferred_element_type=jnp.float32)
        from_imag = jnp.dot(cross[1], table[...], preferred_element_type=jnp.float32)
        rim = jnp.dot(fold[...], edge[...], preferred_element_type=jnp.float32)
        sums = [None] * 9
        for v in range(STACK):
            at = slice(v * pairs, (v + 1) * pairs)
            p, r = from_real[at, :HALF], from_real[at, HALF:]
            s, q = from_imag[at, :HALF], from_imag[at, HALF:]
            terms = []
            for real, imag in ((p - q, r + s), (p + q, s - r), (rim[at, :LANES], rim[at, LANES:])):
                scale = lax.rsqrt(jnp.maximum(real * real + imag * imag, 0.25))
                terms += [real, real * scale, imag * scale]
            sums = terms if v == 0 else [a + b for a, b in zip(sums, terms)]
        for k in range(6):
            total[k] += sums[k]
        for k in range(3):
            edges[k] += sums[6 + k]
        return carry

    lax.fori_loop(0, windows // STACK, step, 0)

    scales = (32766.0 / (PEAK * windows), 32000.0 / windows, 32000.0 / windows)
    wide = LAGS // parts

    def piece(z):
        if z < parts // 2:
            return 1, (parts // 2 - 1 - z) * wide
        return 0, (z - parts // 2) * wide

    lane = lax.broadcasted_iota(jnp.int32, (pairs, LANES), 1)
    last = jnp.zeros((pairs, LANES), jnp.float32)
    for z in range(parts):
        side, start = piece(z)
        for k in range(3):
            if start + wide < HALF:
                column = total[3 * side + k, :, start + wide:start + wide + 1]
            else:
                column = edges[k, :, side:side + 1]
            last = jnp.where(lane == 4 * z + k, column * scales[k], last)
        last = jnp.where(lane == 4 * z + 3, counts[:, 0:1], last)
    turned = jnp.transpose(last)

    def whole(value):
        return jnp.round(value).astype(jnp.int32).astype(jnp.int16)

    for here in range(parts):
        @pl.when(me == here)
        def _():
            for d in range(parts):
                z = here ^ d
                side, start = piece(z)
                for k in range(3):
                    part = total[3 * side + k, :, start:start + wide] * scales[k]
                    outs[d][k * pairs:(k + 1) * pairs, 0:wide] = whole(part)
                tail = turned[4 * z:4 * z + 4]
                tail = jnp.concatenate([tail, jnp.zeros((EXTRA - 4, pairs), jnp.float32)], axis=0)
                outs[d][3 * pairs:3 * pairs + EXTRA, 0:pairs] = whole(tail)


def unit(stations, parts, own, others, name):
    rows = own.shape[0]
    windows = rows // stations
    pairs = stations * stations
    choose = len(others) == 2
    shape = jax.ShapeDtypeStruct((3 * pairs + EXTRA, LANES), jnp.int16)
    return pl.pallas_call(
        functools.partial(unit_kernel, stations, windows, parts, choose),
        out_shape=[shape] * parts,
        scratch_shapes=[
            pltpu.VMEM((windows, stations, 2 * F), jnp.float32),
            pltpu.VMEM((windows, stations, 2 * F), jnp.float32),
            pltpu.VMEM((windows, stations, LANES), jnp.float32),
            pltpu.VMEM((windows, stations, LANES), jnp.float32),
            pltpu.VMEM((2, STACK * pairs, F), jnp.bfloat16),
            pltpu.VMEM((STACK * pairs, 4 * LANES), jnp.bfloat16),
            pltpu.VMEM((6, pairs, HALF), jnp.float32),
            pltpu.VMEM((3, pairs, LANES), jnp.float32),
            pltpu.VMEM((pairs, LANES), jnp.float32),
        ],
        compiler_params=pltpu.CompilerParams(vmem_limit_bytes=48 * 1024 * 1024),
        cost_estimate=pl.CostEstimate(
            flops=4 * rows * stations * F * LAGS, bytes_accessed=3 << 20, transcendentals=rows * stations * LAGS
        ),
        name=name,
    )(own, *others, jnp.asarray(inverse_table()), jnp.asarray(edge_table()))


def finish_kernel(stations, windows, parts, back, *refs):
    sums = refs[:parts]
    outs = refs[parts:]
    pairs = stations * stations
    wide = LAGS // parts
    me = lax.axis_index("win")
    acc = sums[0][...].astype(jnp.int32).astype(jnp.float32)
    for ref in sums[1:]:
        acc = acc + ref[...].astype(jnp.int32).astype(jnp.float32)
    scales = (PEAK * windows / 32766.0, windows / 32000.0, windows / 32000.0)
    tail = jnp.transpose(acc[3 * pairs:])[:pairs]
    inverse = 1.0 / jnp.maximum(tail[:, 3:4], 1.0)

    def stack(linear, real, imag):
        linear = linear * scales[0] * inverse
        real = real * scales[1] * inverse
        imag = imag * scales[2] * inverse
        return linear * (real * real + imag * imag)

    plain = stack(acc[:pairs], acc[pairs:2 * pairs], acc[2 * pairs:3 * pairs])
    edge = stack(tail[:, 0:1], tail[:, 1:2], tail[:, 2:3])
    row = lax.broadcasted_iota(jnp.int32, (LANES, LANES), 0)
    column = lax.broadcasted_iota(jnp.int32, (LANES, LANES), 1)
    mirror = jnp.where((row + column == wide) & (column > 0) & (column < wide), 1.0, 0.0)
    turned = jnp.dot(plain, mirror, precision=lax.Precision.HIGHEST, preferred_element_type=jnp.float32)
    lane = lax.broadcasted_iota(jnp.int32, (pairs, LANES), 1)
    turned = jnp.where(lane == 0, edge, turned)
    negative = me < parts // 2
    outs[0][...] = jnp.where(negative, turned, plain)
    if back:
        value = jnp.where(negative, plain, turned)
        row = lax.broadcasted_iota(jnp.int32, (pairs, pairs), 0)
        column = lax.broadcasted_iota(jnp.int32, (pairs, pairs), 1)
        swap = (row // stations == column % stations) & (row % stations == column // stations)
        swap = jnp.where(swap, 1.0, 0.0)
        outs[1][...] = jnp.dot(swap, value, precision=lax.Precision.HIGHEST, preferred_element_type=jnp.float32)


def finish(stations, windows, sums, back, name):
    pairs = stations * stations
    parts = len(sums)
    shape = jax.ShapeDtypeStruct((pairs, LANES), jnp.float32)
    return pl.pallas_call(
        functools.partial(finish_kernel, stations, windows, parts, back),
        out_shape=[shape] * (2 if back else 1),
        compiler_params=pltpu.CompilerParams(vmem_limit_bytes=16 * 1024 * 1024),
        cost_estimate=pl.CostEstimate(flops=1 << 22, bytes_accessed=1 << 18, transcendentals=0),
        name=name,
    )(*sums)


def exchange(sums):
    parts = len(sums)
    return [sums[0]] + [
        lax.ppermute(sums[d], "win", [(i, i ^ d) for i in range(parts)]) for d in range(1, parts)
    ]


def local(traces, gap_mask, pair_mask):
    blocks = lax.axis_size("sta")
    parts = lax.axis_size("win")
    stations, windows, _ = traces.shape
    white = forward(traces, gap_mask)
    second = lax.ppermute(white, "sta", [((i + 2) % blocks, i) for i in range(blocks)])
    beside = lax.ppermute(white, "sta", [(i ^ 1, i) for i in range(blocks)])
    self_sums = exchange(unit(stations, parts, white, [white], "stack0"))
    handed = lax.ppermute(second, "sta", [(i ^ 1, i) for i in range(blocks)])
    far_sums = exchange(unit(stations, parts, white, [second], "stack2"))
    near_sums = exchange(unit(stations, parts, white, [beside, handed], "stack1"))

    def returned(value, distance):
        route = []
        for b in range(blocks):
            for z in range(parts):
                route.append((b * parts + z, ((b + distance) % blocks) * parts + parts - 1 - z))
        return lax.ppermute(value, ("sta", "win"), route)

    (middle,) = finish(stations, windows, self_sums, False, "finish0")
    far, far_back = finish(stations, windows, far_sums, True, "finish2")
    far_back = returned(far_back, 2)
    near, near_back = finish(stations, windows, near_sums, True, "finish1")
    near_back = returned(near_back, 1)
    wide = LAGS // parts
    pws = jnp.stack(
        [value.reshape(stations, stations, LANES)[..., :wide] for value in (far_back, near_back, middle, near, far)], axis=1
    )
    return pws * pair_mask.astype(jnp.float32)[..., None]


def solution(mesh):
    return jax.shard_map(
        local,
        mesh=mesh,
        in_specs=(P("sta", "win", None), P("sta", "win"), P("sta", None, None)),
        out_specs=P("sta", None, None, "win"),
        check_vma=False,
    )
```

```python
import functools
import math

import jax
import jax.numpy as jnp
import ml_dtypes
import numpy as np
from jax import lax
from jax.experimental import pallas as pl
from jax.experimental.pallas import tpu as pltpu
from jax.sharding import PartitionSpec as P

SAMPLES = 2048
F = 1024
LAGS = 512
WBLK = 128
REACH = 2
LANES = 128
SLICES = F // LANES
HALF = LAGS // 2
PEAK = 34.0
EXTRA = 16
STACK = 8


def bins():
    m = np.arange(LANES // 2)
    rows = [np.concatenate([16 * m, 8 + 16 * m])]
    for s in range(1, SLICES):
        rows.append(np.concatenate([s + 16 * m, 16 - s + 16 * m]))
    return np.stack(rows)


def forward_table():
    at = bins()
    t = np.arange(LANES)
    upper = (np.arange(LANES) >= LANES // 2)[None, :]
    tables = []
    for s in range(SLICES):
        angle = 2.0 * np.pi * ((t[:, None] * at[s][None, :]) % SAMPLES) / SAMPLES
        c, n = np.cos(angle), np.sin(angle)
        if s == 0:
            first = np.concatenate([np.where(upper, 0.0, c), np.where(upper, 0.0, -n)], axis=1)
            second = np.concatenate([np.where(upper, c, 0.0), np.where(upper, -n, 0.0)], axis=1)
        else:
            first = np.concatenate([c, -n], axis=1)
            second = np.concatenate([np.where(upper, -n, n), np.where(upper, -c, c)], axis=1)
        tables.append(np.concatenate([first, second], axis=0))
    return np.stack(tables).astype(ml_dtypes.bfloat16)


def inverse_table():
    at = bins().reshape(-1)
    tau = np.arange(HALF)
    angle = (((at[:, None] * tau[None, :]) % SAMPLES).astype(np.float32)) * np.float32(2.0 * math.pi / SAMPLES)
    both = np.concatenate([np.cos(angle), np.sin(angle)], axis=1).astype(np.float32)
    return (both * np.float32(1.0 / math.sqrt(F))).astype(ml_dtypes.bfloat16)


def edge_table():
    scale = 1.0 / math.sqrt(F)
    sign = np.where(np.arange(LANES) < LANES // 2, 1.0, -1.0) * scale
    table = np.zeros((4 * LANES, 2 * LANES))
    cr, sr, ci, si = (slice(k * LANES, (k + 1) * LANES) for k in range(4))
    table[cr, 0], table[si, 0] = scale, -sign
    table[cr, 1], table[si, 1] = scale, sign
    table[sr, LANES], table[ci, LANES] = sign, scale
    table[sr, LANES + 1], table[ci, LANES + 1] = -sign, scale
    return table.astype(ml_dtypes.bfloat16)


ROOT = float(np.float32(ml_dtypes.bfloat16(math.sqrt(0.5))))


def stage_one(x):
    r = math.sqrt(0.5)
    a = [x[s] + x[s + 8] for s in range(8)]
    b = [x[s] - x[s + 8] for s in range(8)]
    c = [a[s] + a[s + 4] for s in range(4)]
    d = [a[s] - a[s + 4] for s in range(4)]
    e0, e1, g0, g1 = c[0] + c[2], c[1] + c[3], c[0] - c[2], c[1] - c[3]
    pairs = [None] * 8
    pairs[0] = (e0 + e1, e0 - e1)
    pairs[4] = (g0, -g1)
    near, far = r * (d[1] - d[3]), r * (d[1] + d[3])
    pairs[2] = (d[0] + near, -(d[2] + far))
    pairs[6] = (d[0] - near, d[2] - far)
    u = [None] + [b[s] - b[8 - s] for s in (1, 2, 3)]
    v = [None] + [b[s] + b[8 - s] for s in (1, 2, 3)]
    for k in (1, 3, 5, 7):
        real = b[0]
        imag = b[4] * math.sin(math.pi * k / 2)
        for s in (1, 2, 3):
            real = real + u[s] * math.cos(math.pi * s * k / 8)
            imag = imag + v[s] * math.sin(math.pi * s * k / 8)
        pairs[k] = (real, -imag)
    return pairs


def forward_kernel(stations, windows, signs, flags, table, out, first, second):
    rows = stations * windows
    for start in range(0, rows, 16):
        x = signs[start:start + 16, :].astype(jnp.float32)
        y = stage_one([x[:, s * LANES:(s + 1) * LANES] for s in range(16)])
        for s in range(SLICES):
            both = jnp.concatenate(y[s], axis=1)
            top = both.astype(jnp.bfloat16)
            first[s, start:start + 16, :] = top
            second[s, start:start + 16, :] = (both - top.astype(jnp.float32)).astype(jnp.bfloat16)
    spectra = []
    power = jnp.zeros((rows, LANES), jnp.float32)
    for s in range(SLICES):
        z = jnp.dot(first[s], table[s], preferred_element_type=jnp.float32)
        z += jnp.dot(second[s], table[s], preferred_element_type=jnp.float32)
        spectra.append(z)
        power += z[:, :LANES] * z[:, :LANES] + z[:, LANES:] * z[:, LANES:]
    row = lax.broadcasted_iota(jnp.int32, (LANES, LANES), 0) % (LANES // 2) // (WBLK // 16)
    column = lax.broadcasted_iota(jnp.int32, (LANES, LANES), 1) % (LANES // 2) // (WBLK // 16)
    band = jnp.where(row == column, 1.0, 0.0)
    bands = jnp.dot(power, band, precision=lax.Precision.HIGHEST, preferred_element_type=jnp.float32)
    factor = lax.rsqrt(bands * (1.0 / WBLK) + 1e-05)
    keep = jnp.concatenate(
        [jnp.broadcast_to(flags[:, w:w + 1], (stations, LANES)) for w in range(windows)], axis=0
    )
    corner = lax.broadcasted_iota(jnp.int32, (rows, LANES), 1) == 0
    to = lax.broadcasted_iota(jnp.int32, (rows, rows), 0)
    source = lax.broadcasted_iota(jnp.int32, (rows, rows), 1)
    moved = (to // stations == source % windows) & (to % stations == source // windows)
    moved = jnp.where(moved, 1.0, 0.0).astype(jnp.bfloat16)
    factor = jnp.concatenate([factor, factor], axis=1)
    keep = jnp.concatenate([keep, keep], axis=1)
    for s in range(SLICES):
        white = (spectra[s] * factor).astype(jnp.bfloat16)
        white = jnp.dot(moved, white, preferred_element_type=jnp.float32) * keep
        real, imag = white[:, :LANES], white[:, LANES:]
        if s == 0:
            imag = jnp.where(corner, keep[:, :LANES], imag)
        out[:, s * LANES:(s + 1) * LANES] = real.astype(jnp.bfloat16)
        out[:, F + s * LANES:F + (s + 1) * LANES] = imag.astype(jnp.bfloat16)


def forward(traces, gaps):
    stations, windows, samples = traces.shape
    rows = stations * windows
    signs = jnp.sign(traces.reshape(rows, samples)).astype(jnp.bfloat16)
    table = jnp.asarray(forward_table()) * lax.optimization_barrier(jnp.ones((), jnp.bfloat16))
    return pl.pallas_call(
        functools.partial(forward_kernel, stations, windows),
        out_shape=jax.ShapeDtypeStruct((rows, 2 * F), jnp.bfloat16),
        scratch_shapes=[
            pltpu.VMEM((SLICES, rows, 2 * LANES), jnp.bfloat16),
            pltpu.VMEM((SLICES, rows, 2 * LANES), jnp.bfloat16),
        ],
        compiler_params=pltpu.CompilerParams(vmem_limit_bytes=16 * 1024 * 1024),
        cost_estimate=pl.CostEstimate(flops=6 * rows * F * 512, bytes_accessed=4 << 20, transcendentals=rows * LANES),
        name="whiten",
    )(signs, gaps.astype(jnp.float32), table)


def unit_kernel(stations, windows, parts, choose, *refs):
    x_ref, refs = refs[0], refs[1:]
    y_refs, refs = refs[:2 if choose else 1], refs[2 if choose else 1:]
    table, edge = refs[:2]
    outs = refs[2:2 + parts]
    xf, yf, x0, y0, cross, fold, total, edges, counts = refs[2 + parts:]
    pairs = stations * stations
    rows = stations * windows
    me = lax.axis_index("win")

    def load(source, target, corner):
        lane = lax.broadcasted_iota(jnp.int32, (rows, LANES), 1) == 0
        for s in range(2 * SLICES):
            at = slice(s * LANES, (s + 1) * LANES)
            value = source[:, at].astype(jnp.float32)
            if s == SLICES:
                corner[...] = value.reshape(corner.shape)
                value = jnp.where(lane, 0.0, value)
            target[:, :, at] = value.reshape(windows, stations, LANES)

    load(x_ref, xf, x0)
    if choose:
        odd = lax.rem(lax.axis_index("sta"), 2)

        @pl.when(odd == 0)
        def _():
            load(y_refs[0], yf, y0)

        @pl.when(odd == 1)
        def _():
            load(y_refs[1], yf, y0)
    else:
        load(y_refs[0], yf, y0)

    total[...] = jnp.zeros_like(total)
    edges[...] = jnp.zeros_like(edges)
    counts[...] = jnp.zeros_like(counts)

    def step(chunk, carry):
        for v in range(STACK):
            w = chunk * STACK + v
            for i in range(0, stations, 2):
                folded = [[], [], [], []]
                for e in range(2):
                    at = pl.ds((i + e) * stations, stations)
                    counts[at, :] += x0[w, i + e:i + e + 1, :] * y0[w]
                spot = pl.ds(v * pairs + i * stations, 2 * stations)
                reals, imags = [], []
                for s in range(SLICES):
                    re = slice(s * LANES, (s + 1) * LANES)
                    im = slice(F + s * LANES, F + (s + 1) * LANES)
                    yr, yi = yf[w, :, re], yf[w, :, im]
                    halves = []
                    for e in range(2):
                        xr, xi = xf[w, i + e:i + e + 1, re], xf[w, i + e:i + e + 1, im]
                        halves.append((xr * yr + xi * yi, xi * yr - xr * yi))
                    cr = jnp.concatenate([h[0] for h in halves], axis=0)
                    ci = jnp.concatenate([h[1] for h in halves], axis=0)
                    reals.append(cr)
                    imags.append(ci)
                    cross[0, spot, re] = cr.astype(jnp.bfloat16)
                    cross[1, spot, re] = ci.astype(jnp.bfloat16)
                for k, c in enumerate((reals, imags)):
                    cosine = (c[0] - c[4]) + ROOT * ((c[1] + c[7]) - (c[3] + c[5]))
                    sine = (c[2] - c[6]) + ROOT * ((c[1] + c[3]) - (c[5] + c[7]))
                    fold[spot, 2 * k * LANES:(2 * k + 1) * LANES] = cosine.astype(jnp.bfloat16)
                    fold[spot, (2 * k + 1) * LANES:(2 * k + 2) * LANES] = sine.astype(jnp.bfloat16)
        from_real = jnp.dot(cross[0], table[...], preferred_element_type=jnp.float32)
        from_imag = jnp.dot(cross[1], table[...], preferred_element_type=jnp.float32)
        rim = jnp.dot(fold[...], edge[...], preferred_element_type=jnp.float32)
        sums = [None] * 9
        for v in range(STACK):
            at = slice(v * pairs, (v + 1) * pairs)
            p, r = from_real[at, :HALF], from_real[at, HALF:]
            s, q = from_imag[at, :HALF], from_imag[at, HALF:]
            terms = []
            for real, imag in ((p - q, r + s), (p + q, s - r), (rim[at, :LANES], rim[at, LANES:])):
                scale = lax.rsqrt(jnp.maximum(real * real + imag * imag, 0.25))
                terms += [real, real * scale, imag * scale]
            sums = terms if v == 0 else [a + b for a, b in zip(sums, terms)]
        for k in range(6):
            total[k] += sums[k]
        for k in range(3):
            edges[k] += sums[6 + k]
        return carry

    lax.fori_loop(0, windows // STACK, step, 0)

    scales = (32766.0 / (PEAK * windows), 32000.0 / windows, 32000.0 / windows)
    wide = LAGS // parts

    def piece(z):
        if z < parts // 2:
            return 1, (parts // 2 - 1 - z) * wide
        return 0, (z - parts // 2) * wide

    lane = lax.broadcasted_iota(jnp.int32, (pairs, LANES), 1)
    last = jnp.zeros((pairs, LANES), jnp.float32)
    for z in range(parts):
        side, start = piece(z)
        for k in range(3):
            if start + wide < HALF:
                column = total[3 * side + k, :, start + wide:start + wide + 1]
            else:
                column = edges[k, :, side:side + 1]
            last = jnp.where(lane == 4 * z + k, column * scales[k], last)
        last = jnp.where(lane == 4 * z + 3, counts[:, 0:1], last)
    turned = jnp.transpose(last)

    def whole(value):
        return jnp.round(value).astype(jnp.int32).astype(jnp.int16)

    for here in range(parts):
        @pl.when(me == here)
        def _():
            for d in range(parts):
                z = here ^ d
                side, start = piece(z)
                for k in range(3):
                    part = total[3 * side + k, :, start:start + wide] * scales[k]
                    outs[d][k * pairs:(k + 1) * pairs, 0:wide] = whole(part)
                tail = turned[4 * z:4 * z + 4]
                tail = jnp.concatenate([tail, jnp.zeros((EXTRA - 4, pairs), jnp.float32)], axis=0)
                outs[d][3 * pairs:3 * pairs + EXTRA, 0:pairs] = whole(tail)


def unit(stations, parts, own, others, name):
    rows = own.shape[0]
    windows = rows // stations
    pairs = stations * stations
    choose = len(others) == 2
    shape = jax.ShapeDtypeStruct((3 * pairs + EXTRA, LANES), jnp.int16)
    return pl.pallas_call(
        functools.partial(unit_kernel, stations, windows, parts, choose),
        out_shape=[shape] * parts,
        scratch_shapes=[
            pltpu.VMEM((windows, stations, 2 * F), jnp.float32),
            pltpu.VMEM((windows, stations, 2 * F), jnp.float32),
            pltpu.VMEM((windows, stations, LANES), jnp.float32),
            pltpu.VMEM((windows, stations, LANES), jnp.float32),
            pltpu.VMEM((2, STACK * pairs, F), jnp.bfloat16),
            pltpu.VMEM((STACK * pairs, 4 * LANES), jnp.bfloat16),
            pltpu.VMEM((6, pairs, HALF), jnp.float32),
            pltpu.VMEM((3, pairs, LANES), jnp.float32),
            pltpu.VMEM((pairs, LANES), jnp.float32),
        ],
        compiler_params=pltpu.CompilerParams(vmem_limit_bytes=24 * 1024 * 1024),
        cost_estimate=pl.CostEstimate(
            flops=4 * rows * stations * F * LAGS, bytes_accessed=3 << 20, transcendentals=rows * stations * LAGS
        ),
        name=name,
    )(own, *others, jnp.asarray(inverse_table()), jnp.asarray(edge_table()))


def finish_kernel(stations, windows, parts, back, *refs):
    sums = refs[:parts]
    outs = refs[parts:]
    pairs = stations * stations
    wide = LAGS // parts
    negative = lax.axis_index("win") < parts // 2
    everything = sums[0][...].astype(jnp.int32).astype(jnp.float32)
    for ref in sums[1:]:
        everything = everything + ref[...].astype(jnp.int32).astype(jnp.float32)
    scales = (PEAK * windows / 32766.0, windows / 32000.0, windows / 32000.0)
    row = lax.broadcasted_iota(jnp.int32, (LANES, LANES), 0)
    column = lax.broadcasted_iota(jnp.int32, (LANES, LANES), 1)
    mirror = jnp.where((row + column == wide) & (column > 0) & (column < wide), 1.0, 0.0)
    lane = lax.broadcasted_iota(jnp.int32, (pairs, LANES), 1)
    row = lax.broadcasted_iota(jnp.int32, (pairs, pairs), 0)
    column = lax.broadcasted_iota(jnp.int32, (pairs, pairs), 1)
    swap = (row // stations == column % stations) & (row % stations == column // stations)
    swap = jnp.where(swap, 1.0, 0.0)
    if True:
        acc = everything
        tail = jnp.transpose(acc[3 * pairs:])[:pairs]
        inverse = 1.0 / jnp.maximum(tail[:, 3:4], 1.0)

        def stack(linear, real, imag):
            linear = linear * scales[0] * inverse
            real = real * scales[1] * inverse
            imag = imag * scales[2] * inverse
            return linear * (real * real + imag * imag)

        plain = stack(acc[:pairs], acc[pairs:2 * pairs], acc[2 * pairs:3 * pairs])
        edge = stack(tail[:, 0:1], tail[:, 1:2], tail[:, 2:3])
        turned = jnp.dot(plain, mirror, precision=lax.Precision.HIGHEST, preferred_element_type=jnp.float32)
        turned = jnp.where(lane == 0, edge, turned)
        outs[0][...] = jnp.where(negative, turned, plain)
        if back:
            value = jnp.where(negative, plain, turned)
            outs[1][...] = jnp.dot(
                swap, value, precision=lax.Precision.HIGHEST, preferred_element_type=jnp.float32
            )


def finish(stations, windows, sums, back, name):
    pairs = stations * stations
    parts = len(sums)
    shape = jax.ShapeDtypeStruct((pairs, LANES), jnp.float32)
    return pl.pallas_call(
        functools.partial(finish_kernel, stations, windows, parts, back),
        out_shape=[shape] * (2 if back else 1),
        compiler_params=pltpu.CompilerParams(vmem_limit_bytes=16 * 1024 * 1024),
        cost_estimate=pl.CostEstimate(flops=1 << 22, bytes_accessed=1 << 18, transcendentals=0),
        name=name,
    )(*sums)


def exchange(sums):
    parts = len(sums)
    return [sums[0]] + [
        lax.ppermute(sums[d], "win", [(i, i ^ d) for i in range(parts)]) for d in range(1, parts)
    ]


def local(traces, gap_mask, pair_mask):
    blocks = lax.axis_size("sta")
    parts = lax.axis_size("win")
    stations, windows, _ = traces.shape
    white = forward(traces, gap_mask)
    second = lax.ppermute(white, "sta", [((i + 2) % blocks, i) for i in range(blocks)])
    beside = lax.ppermute(white, "sta", [(i ^ 1, i) for i in range(blocks)])
    own_sums = exchange(unit(stations, parts, white, [white], "stack0"))
    (middle,) = finish(stations, windows, own_sums, False, "finish0")
    second, middle = lax.optimization_barrier((second, middle))
    handed = lax.ppermute(second, "sta", [(i ^ 1, i) for i in range(blocks)])
    far_sums = exchange(unit(stations, parts, white, [second], "stack2"))
    near_sums = exchange(unit(stations, parts, white, [beside, handed], "stack1"))

    def returned(value, distance):
        route = []
        for b in range(blocks):
            for z in range(parts):
                route.append((b * parts + z, ((b + distance) % blocks) * parts + parts - 1 - z))
        return lax.ppermute(value, ("sta", "win"), route)

    far, far_back = finish(stations, windows, far_sums, True, "finish2")
    far_back = returned(far_back, 2)
    near, near_back = finish(stations, windows, near_sums, True, "finish1")
    near_back = returned(near_back, 1)
    wide = LAGS // parts
    pws = jnp.stack(
        [value.reshape(stations, stations, LANES)[..., :wide] for value in (far_back, near_back, middle, near, far)], axis=1
    )
    return pws * pair_mask.astype(jnp.float32)[..., None]


def solution(mesh):
    return jax.shard_map(
        local,
        mesh=mesh,
        in_specs=(P("sta", "win", None), P("sta", "win"), P("sta", None, None)),
        out_specs=P("sta", None, None, "win"),
        check_vma=False,
    )
```

```python
import functools
import math

import jax
import jax.numpy as jnp
import ml_dtypes
import numpy as np
from jax import lax
from jax.experimental import pallas as pl
from jax.experimental.pallas import tpu as pltpu
from jax.sharding import PartitionSpec as P

SAMPLES = 2048
F = 1024
LAGS = 512
WBLK = 128
REACH = 2
LANES = 128
SLICES = F // LANES
HALF = LAGS // 2
PEAK = 34.0
EXTRA = 16
STACK = 16


def bins():
    m = np.arange(LANES // 2)
    rows = [np.concatenate([16 * m, 8 + 16 * m])]
    for s in range(1, SLICES):
        rows.append(np.concatenate([s + 16 * m, 16 - s + 16 * m]))
    return np.stack(rows)


def forward_table():
    at = bins()
    t = np.arange(LANES)
    upper = (np.arange(LANES) >= LANES // 2)[None, :]
    tables = []
    for s in range(SLICES):
        angle = 2.0 * np.pi * ((t[:, None] * at[s][None, :]) % SAMPLES) / SAMPLES
        c, n = np.cos(angle), np.sin(angle)
        if s == 0:
            first = np.concatenate([np.where(upper, 0.0, c), np.where(upper, 0.0, -n)], axis=1)
            second = np.concatenate([np.where(upper, c, 0.0), np.where(upper, -n, 0.0)], axis=1)
        else:
            first = np.concatenate([c, -n], axis=1)
            second = np.concatenate([np.where(upper, -n, n), np.where(upper, -c, c)], axis=1)
        tables.append(np.concatenate([first, second], axis=0))
    return np.stack(tables).astype(ml_dtypes.bfloat16)


def inverse_table():
    at = bins().reshape(-1)
    tau = np.arange(HALF)
    angle = (((at[:, None] * tau[None, :]) % SAMPLES).astype(np.float32)) * np.float32(2.0 * math.pi / SAMPLES)
    both = np.concatenate([np.cos(angle), np.sin(angle)], axis=1).astype(np.float32)
    return (both * np.float32(1.0 / math.sqrt(F))).astype(ml_dtypes.bfloat16)


def edge_table():
    scale = 1.0 / math.sqrt(F)
    sign = np.where(np.arange(LANES) < LANES // 2, 1.0, -1.0) * scale
    table = np.zeros((4 * LANES, 2 * LANES))
    cr, sr, ci, si = (slice(k * LANES, (k + 1) * LANES) for k in range(4))
    table[cr, 0], table[si, 0] = scale, -sign
    table[cr, 1], table[si, 1] = scale, sign
    table[sr, LANES], table[ci, LANES] = sign, scale
    table[sr, LANES + 1], table[ci, LANES + 1] = -sign, scale
    return table.astype(ml_dtypes.bfloat16)


ROOT = float(np.float32(ml_dtypes.bfloat16(math.sqrt(0.5))))


def stage_one(x):
    r = math.sqrt(0.5)
    a = [x[s] + x[s + 8] for s in range(8)]
    b = [x[s] - x[s + 8] for s in range(8)]
    c = [a[s] + a[s + 4] for s in range(4)]
    d = [a[s] - a[s + 4] for s in range(4)]
    e0, e1, g0, g1 = c[0] + c[2], c[1] + c[3], c[0] - c[2], c[1] - c[3]
    pairs = [None] * 8
    pairs[0] = (e0 + e1, e0 - e1)
    pairs[4] = (g0, -g1)
    near, far = r * (d[1] - d[3]), r * (d[1] + d[3])
    pairs[2] = (d[0] + near, -(d[2] + far))
    pairs[6] = (d[0] - near, d[2] - far)
    u = [None] + [b[s] - b[8 - s] for s in (1, 2, 3)]
    v = [None] + [b[s] + b[8 - s] for s in (1, 2, 3)]
    for k in (1, 3, 5, 7):
        real = b[0]
        imag = b[4] * math.sin(math.pi * k / 2)
        for s in (1, 2, 3):
            real = real + u[s] * math.cos(math.pi * s * k / 8)
            imag = imag + v[s] * math.sin(math.pi * s * k / 8)
        pairs[k] = (real, -imag)
    return pairs


def forward_kernel(stations, windows, signs, flags, table, out, first, second):
    rows = stations * windows
    for start in range(0, rows, 16):
        x = signs[start:start + 16, :].astype(jnp.float32)
        y = stage_one([x[:, s * LANES:(s + 1) * LANES] for s in range(16)])
        for s in range(SLICES):
            both = jnp.concatenate(y[s], axis=1)
            top = both.astype(jnp.bfloat16)
            first[s, start:start + 16, :] = top
            second[s, start:start + 16, :] = (both - top.astype(jnp.float32)).astype(jnp.bfloat16)
    spectra = []
    power = jnp.zeros((rows, LANES), jnp.float32)
    for s in range(SLICES):
        z = jnp.dot(first[s], table[s], preferred_element_type=jnp.float32)
        z += jnp.dot(second[s], table[s], preferred_element_type=jnp.float32)
        spectra.append(z)
        power += z[:, :LANES] * z[:, :LANES] + z[:, LANES:] * z[:, LANES:]
    row = lax.broadcasted_iota(jnp.int32, (LANES, LANES), 0) % (LANES // 2) // (WBLK // 16)
    column = lax.broadcasted_iota(jnp.int32, (LANES, LANES), 1) % (LANES // 2) // (WBLK // 16)
    band = jnp.where(row == column, 1.0, 0.0)
    bands = jnp.dot(power, band, precision=lax.Precision.HIGHEST, preferred_element_type=jnp.float32)
    factor = lax.rsqrt(bands * (1.0 / WBLK) + 1e-05)
    keep = jnp.concatenate(
        [jnp.broadcast_to(flags[:, w:w + 1], (stations, LANES)) for w in range(windows)], axis=0
    )
    corner = lax.broadcasted_iota(jnp.int32, (rows, LANES), 1) == 0
    to = lax.broadcasted_iota(jnp.int32, (rows, rows), 0)
    source = lax.broadcasted_iota(jnp.int32, (rows, rows), 1)
    moved = (to // stations == source % windows) & (to % stations == source // windows)
    moved = jnp.where(moved, 1.0, 0.0).astype(jnp.bfloat16)
    factor = jnp.concatenate([factor, factor], axis=1)
    keep = jnp.concatenate([keep, keep], axis=1)
    for s in range(SLICES):
        white = (spectra[s] * factor).astype(jnp.bfloat16)
        white = jnp.dot(moved, white, preferred_element_type=jnp.float32) * keep
        real, imag = white[:, :LANES], white[:, LANES:]
        if s == 0:
            imag = jnp.where(corner, keep[:, :LANES], imag)
        out[:, s * LANES:(s + 1) * LANES] = real.astype(jnp.bfloat16)
        out[:, F + s * LANES:F + (s + 1) * LANES] = imag.astype(jnp.bfloat16)


def forward(traces, gaps):
    stations, windows, samples = traces.shape
    rows = stations * windows
    signs = jnp.sign(traces.reshape(rows, samples)).astype(jnp.bfloat16)
    table = jnp.asarray(forward_table()) * lax.optimization_barrier(jnp.ones((), jnp.bfloat16))
    return pl.pallas_call(
        functools.partial(forward_kernel, stations, windows),
        out_shape=jax.ShapeDtypeStruct((rows, 2 * F), jnp.bfloat16),
        scratch_shapes=[
            pltpu.VMEM((SLICES, rows, 2 * LANES), jnp.bfloat16),
            pltpu.VMEM((SLICES, rows, 2 * LANES), jnp.bfloat16),
        ],
        compiler_params=pltpu.CompilerParams(vmem_limit_bytes=16 * 1024 * 1024),
        cost_estimate=pl.CostEstimate(flops=6 * rows * F * 512, bytes_accessed=4 << 20, transcendentals=rows * LANES),
        name="whiten",
    )(signs, gaps.astype(jnp.float32), table)


def unit_kernel(stations, windows, parts, choose, *refs):
    x_ref, refs = refs[0], refs[1:]
    y_refs, refs = refs[:2 if choose else 1], refs[2 if choose else 1:]
    table, edge = refs[:2]
    outs = refs[2:2 + parts]
    xf, yf, x0, y0, cross, fold, total, edges, counts = refs[2 + parts:]
    pairs = stations * stations
    rows = stations * windows
    me = lax.axis_index("win")

    def load(source, target, corner):
        lane = lax.broadcasted_iota(jnp.int32, (rows, LANES), 1) == 0
        for s in range(2 * SLICES):
            at = slice(s * LANES, (s + 1) * LANES)
            value = source[:, at].astype(jnp.float32)
            if s == SLICES:
                corner[...] = value.reshape(corner.shape)
                value = jnp.where(lane, 0.0, value)
            target[:, :, at] = value.reshape(windows, stations, LANES)

    load(x_ref, xf, x0)
    if choose:
        odd = lax.rem(lax.axis_index("sta"), 2)

        @pl.when(odd == 0)
        def _():
            load(y_refs[0], yf, y0)

        @pl.when(odd == 1)
        def _():
            load(y_refs[1], yf, y0)
    else:
        load(y_refs[0], yf, y0)

    total[...] = jnp.zeros_like(total)
    edges[...] = jnp.zeros_like(edges)
    counts[...] = jnp.zeros_like(counts)

    def step(chunk, carry):
        for v in range(STACK):
            w = chunk * STACK + v
            for i in range(0, stations, 2):
                folded = [[], [], [], []]
                for e in range(2):
                    at = pl.ds((i + e) * stations, stations)
                    counts[at, :] += x0[w, i + e:i + e + 1, :] * y0[w]
                spot = pl.ds(v * pairs + i * stations, 2 * stations)
                reals, imags = [], []
                for s in range(SLICES):
                    re = slice(s * LANES, (s + 1) * LANES)
                    im = slice(F + s * LANES, F + (s + 1) * LANES)
                    yr, yi = yf[w, :, re], yf[w, :, im]
                    halves = []
                    for e in range(2):
                        xr, xi = xf[w, i + e:i + e + 1, re], xf[w, i + e:i + e + 1, im]
                        halves.append((xr * yr + xi * yi, xi * yr - xr * yi))
                    cr = jnp.concatenate([h[0] for h in halves], axis=0)
                    ci = jnp.concatenate([h[1] for h in halves], axis=0)
                    reals.append(cr)
                    imags.append(ci)
                    cross[0, spot, re] = cr.astype(jnp.bfloat16)
                    cross[1, spot, re] = ci.astype(jnp.bfloat16)
                for k, c in enumerate((reals, imags)):
                    cosine = (c[0] - c[4]) + ROOT * ((c[1] + c[7]) - (c[3] + c[5]))
                    sine = (c[2] - c[6]) + ROOT * ((c[1] + c[3]) - (c[5] + c[7]))
                    fold[spot, 2 * k * LANES:(2 * k + 1) * LANES] = cosine.astype(jnp.bfloat16)
                    fold[spot, (2 * k + 1) * LANES:(2 * k + 2) * LANES] = sine.astype(jnp.bfloat16)
        from_real = jnp.dot(cross[0], table[...], preferred_element_type=jnp.float32)
        from_imag = jnp.dot(cross[1], table[...], preferred_element_type=jnp.float32)
        rim = jnp.dot(fold[...], edge[...], preferred_element_type=jnp.float32)
        sums = [None] * 9
        for v in range(STACK):
            at = slice(v * pairs, (v + 1) * pairs)
            p, r = from_real[at, :HALF], from_real[at, HALF:]
            s, q = from_imag[at, :HALF], from_imag[at, HALF:]
            terms = []
            for real, imag in ((p - q, r + s), (p + q, s - r), (rim[at, :LANES], rim[at, LANES:])):
                scale = lax.rsqrt(jnp.maximum(real * real + imag * imag, 0.25))
                terms += [real, real * scale, imag * scale]
            sums = terms if v == 0 else [a + b for a, b in zip(sums, terms)]
        for k in range(6):
            total[k] += sums[k]
        for k in range(3):
            edges[k] += sums[6 + k]
        return carry

    lax.fori_loop(0, windows // STACK, step, 0)

    scales = (32766.0 / (PEAK * windows), 32000.0 / windows, 32000.0 / windows)
    wide = LAGS // parts

    def piece(z):
        if z < parts // 2:
            return 1, (parts // 2 - 1 - z) * wide
        return 0, (z - parts // 2) * wide

    lane = lax.broadcasted_iota(jnp.int32, (pairs, LANES), 1)
    last = jnp.zeros((pairs, LANES), jnp.float32)
    for z in range(parts):
        side, start = piece(z)
        for k in range(3):
            if start + wide < HALF:
                column = total[3 * side + k, :, start + wide:start + wide + 1]
            else:
                column = edges[k, :, side:side + 1]
            last = jnp.where(lane == 4 * z + k, column * scales[k], last)
        last = jnp.where(lane == 4 * z + 3, counts[:, 0:1], last)
    turned = jnp.transpose(last)

    def whole(value):
        return jnp.round(value).astype(jnp.int32).astype(jnp.int16)

    for here in range(parts):
        @pl.when(me == here)
        def _():
            for d in range(parts):
                z = here ^ d
                side, start = piece(z)
                for k in range(3):
                    part = total[3 * side + k, :, start:start + wide] * scales[k]
                    outs[d][k * pairs:(k + 1) * pairs, 0:wide] = whole(part)
                tail = turned[4 * z:4 * z + 4]
                tail = jnp.concatenate([tail, jnp.zeros((EXTRA - 4, pairs), jnp.float32)], axis=0)
                outs[d][3 * pairs:3 * pairs + EXTRA, 0:pairs] = whole(tail)


def unit(stations, parts, own, others, name):
    rows = own.shape[0]
    windows = rows // stations
    pairs = stations * stations
    choose = len(others) == 2
    shape = jax.ShapeDtypeStruct((3 * pairs + EXTRA, LANES), jnp.int16)
    return pl.pallas_call(
        functools.partial(unit_kernel, stations, windows, parts, choose),
        out_shape=[shape] * parts,
        scratch_shapes=[
            pltpu.VMEM((windows, stations, 2 * F), jnp.float32),
            pltpu.VMEM((windows, stations, 2 * F), jnp.float32),
            pltpu.VMEM((windows, stations, LANES), jnp.float32),
            pltpu.VMEM((windows, stations, LANES), jnp.float32),
            pltpu.VMEM((2, STACK * pairs, F), jnp.bfloat16),
            pltpu.VMEM((STACK * pairs, 4 * LANES), jnp.bfloat16),
            pltpu.VMEM((6, pairs, HALF), jnp.float32),
            pltpu.VMEM((3, pairs, LANES), jnp.float32),
            pltpu.VMEM((pairs, LANES), jnp.float32),
        ],
        compiler_params=pltpu.CompilerParams(vmem_limit_bytes=24 * 1024 * 1024),
        cost_estimate=pl.CostEstimate(
            flops=4 * rows * stations * F * LAGS, bytes_accessed=3 << 20, transcendentals=rows * stations * LAGS
        ),
        name=name,
    )(own, *others, jnp.asarray(inverse_table()), jnp.asarray(edge_table()))


def finish_kernel(stations, windows, parts, back, *refs):
    sums = refs[:parts]
    outs = refs[parts:]
    pairs = stations * stations
    wide = LAGS // parts
    negative = lax.axis_index("win") < parts // 2
    everything = sums[0][...].astype(jnp.int32).astype(jnp.float32)
    for ref in sums[1:]:
        everything = everything + ref[...].astype(jnp.int32).astype(jnp.float32)
    scales = (PEAK * windows / 32766.0, windows / 32000.0, windows / 32000.0)
    row = lax.broadcasted_iota(jnp.int32, (LANES, LANES), 0)
    column = lax.broadcasted_iota(jnp.int32, (LANES, LANES), 1)
    mirror = jnp.where((row + column == wide) & (column > 0) & (column < wide), 1.0, 0.0)
    lane = lax.broadcasted_iota(jnp.int32, (pairs, LANES), 1)
    row = lax.broadcasted_iota(jnp.int32, (pairs, pairs), 0)
    column = lax.broadcasted_iota(jnp.int32, (pairs, pairs), 1)
    swap = (row // stations == column % stations) & (row % stations == column // stations)
    swap = jnp.where(swap, 1.0, 0.0)
    if True:
        acc = everything
        tail = jnp.transpose(acc[3 * pairs:])[:pairs]
        inverse = 1.0 / jnp.maximum(tail[:, 3:4], 1.0)

        def stack(linear, real, imag):
            linear = linear * scales[0] * inverse
            real = real * scales[1] * inverse
            imag = imag * scales[2] * inverse
            return linear * (real * real + imag * imag)

        plain = stack(acc[:pairs], acc[pairs:2 * pairs], acc[2 * pairs:3 * pairs])
        edge = stack(tail[:, 0:1], tail[:, 1:2], tail[:, 2:3])
        turned = jnp.dot(plain, mirror, precision=lax.Precision.HIGHEST, preferred_element_type=jnp.float32)
        turned = jnp.where(lane == 0, edge, turned)
        outs[0][...] = jnp.where(negative, turned, plain)
        if back:
            value = jnp.where(negative, plain, turned)
            outs[1][...] = jnp.dot(
                swap, value, precision=lax.Precision.HIGHEST, preferred_element_type=jnp.float32
            )


def finish(stations, windows, sums, back, name):
    pairs = stations * stations
    parts = len(sums)
    shape = jax.ShapeDtypeStruct((pairs, LANES), jnp.float32)
    return pl.pallas_call(
        functools.partial(finish_kernel, stations, windows, parts, back),
        out_shape=[shape] * (2 if back else 1),
        compiler_params=pltpu.CompilerParams(vmem_limit_bytes=16 * 1024 * 1024),
        cost_estimate=pl.CostEstimate(flops=1 << 22, bytes_accessed=1 << 18, transcendentals=0),
        name=name,
    )(*sums)


def exchange(sums):
    parts = len(sums)
    return [sums[0]] + [
        lax.ppermute(sums[d], "win", [(i, i ^ d) for i in range(parts)]) for d in range(parts - 1, 0, -1)
    ]


def local(traces, gap_mask, pair_mask):
    blocks = lax.axis_size("sta")
    parts = lax.axis_size("win")
    stations, windows, _ = traces.shape
    white = forward(traces, gap_mask)
    second = lax.ppermute(white, "sta", [((i + 2) % blocks, i) for i in range(blocks)])
    beside = lax.ppermute(white, "sta", [(i ^ 1, i) for i in range(blocks)])
    own_sums = exchange(unit(stations, parts, white, [white], "stack0"))
    (middle,) = finish(stations, windows, own_sums, False, "finish0")
    second, middle = lax.optimization_barrier((second, middle))
    handed = lax.ppermute(second, "sta", [(i ^ 1, i) for i in range(blocks)])
    far_sums = exchange(unit(stations, parts, white, [second], "stack2"))
    near_sums = exchange(unit(stations, parts, white, [beside, handed], "stack1"))

    def returned(value, distance):
        route = []
        for b in range(blocks):
            for z in range(parts):
                route.append((b * parts + z, ((b + distance) % blocks) * parts + parts - 1 - z))
        return lax.ppermute(value, ("sta", "win"), route)

    far, far_back = finish(stations, windows, far_sums, True, "finish2")
    far_back = returned(far_back, 2)
    near, near_back = finish(stations, windows, near_sums, True, "finish1")
    near_back = returned(near_back, 1)
    wide = LAGS // parts
    pws = jnp.stack(
        [value.reshape(stations, stations, LANES)[..., :wide] for value in (far_back, near_back, middle, near, far)], axis=1
    )
    return pws * pair_mask.astype(jnp.float32)[..., None]


def solution(mesh):
    return jax.shard_map(
        local,
        mesh=mesh,
        in_specs=(P("sta", "win", None), P("sta", "win"), P("sta", None, None)),
        out_specs=P("sta", None, None, "win"),
        check_vma=False,
    )
```

```python
import functools
import math

import jax
import jax.numpy as jnp
import ml_dtypes
import numpy as np
from jax import lax
from jax.experimental import pallas as pl
from jax.experimental.pallas import tpu as pltpu
from jax.sharding import PartitionSpec as P

SAMPLES = 2048
F = 1024
LAGS = 512
WBLK = 128
REACH = 2
LANES = 128
SLICES = F // LANES
HALF = LAGS // 2
PEAK = 34.0
EXTRA = 16
STACK = 16


def bins():
    m = np.arange(LANES // 2)
    rows = [np.concatenate([16 * m, 8 + 16 * m])]
    for s in range(1, SLICES):
        rows.append(np.concatenate([s + 16 * m, 16 - s + 16 * m]))
    return np.stack(rows)


def forward_table():
    at = bins()
    t = np.arange(LANES)
    upper = (np.arange(LANES) >= LANES // 2)[None, :]
    tables = []
    for s in range(SLICES):
        angle = 2.0 * np.pi * ((t[:, None] * at[s][None, :]) % SAMPLES) / SAMPLES
        c, n = np.cos(angle), np.sin(angle)
        if s == 0:
            first = np.concatenate([np.where(upper, 0.0, c), np.where(upper, 0.0, -n)], axis=1)
            second = np.concatenate([np.where(upper, c, 0.0), np.where(upper, -n, 0.0)], axis=1)
        else:
            first = np.concatenate([c, -n], axis=1)
            second = np.concatenate([np.where(upper, -n, n), np.where(upper, -c, c)], axis=1)
        tables.append(np.concatenate([first, second], axis=0))
    return np.stack(tables).astype(ml_dtypes.bfloat16)


def inverse_table():
    at = bins().reshape(-1)
    tau = np.arange(HALF)
    angle = (((at[:, None] * tau[None, :]) % SAMPLES).astype(np.float32)) * np.float32(2.0 * math.pi / SAMPLES)
    both = np.concatenate([np.cos(angle), np.sin(angle)], axis=1).astype(np.float32)
    return (both * np.float32(1.0 / math.sqrt(F))).astype(ml_dtypes.bfloat16)


def edge_table():
    scale = 1.0 / math.sqrt(F)
    sign = np.where(np.arange(LANES) < LANES // 2, 1.0, -1.0) * scale
    table = np.zeros((4 * LANES, 2 * LANES))
    cr, sr, ci, si = (slice(k * LANES, (k + 1) * LANES) for k in range(4))
    table[cr, 0], table[si, 0] = scale, -sign
    table[cr, 1], table[si, 1] = scale, sign
    table[sr, LANES], table[ci, LANES] = sign, scale
    table[sr, LANES + 1], table[ci, LANES + 1] = -sign, scale
    return table.astype(ml_dtypes.bfloat16)


ROOT = float(np.float32(ml_dtypes.bfloat16(math.sqrt(0.5))))


def stage_one(x):
    r = math.sqrt(0.5)
    a = [x[s] + x[s + 8] for s in range(8)]
    b = [x[s] - x[s + 8] for s in range(8)]
    c = [a[s] + a[s + 4] for s in range(4)]
    d = [a[s] - a[s + 4] for s in range(4)]
    e0, e1, g0, g1 = c[0] + c[2], c[1] + c[3], c[0] - c[2], c[1] - c[3]
    pairs = [None] * 8
    pairs[0] = (e0 + e1, e0 - e1)
    pairs[4] = (g0, -g1)
    near, far = r * (d[1] - d[3]), r * (d[1] + d[3])
    pairs[2] = (d[0] + near, -(d[2] + far))
    pairs[6] = (d[0] - near, d[2] - far)
    u = [None] + [b[s] - b[8 - s] for s in (1, 2, 3)]
    v = [None] + [b[s] + b[8 - s] for s in (1, 2, 3)]
    for k in (1, 3, 5, 7):
        real = b[0]
        imag = b[4] * math.sin(math.pi * k / 2)
        for s in (1, 2, 3):
            real = real + u[s] * math.cos(math.pi * s * k / 8)
            imag = imag + v[s] * math.sin(math.pi * s * k / 8)
        pairs[k] = (real, -imag)
    return pairs


def forward_kernel(stations, windows, signs, flags, table, out, first, second):
    rows = stations * windows
    for start in range(0, rows, 16):
        x = signs[start:start + 16, :].astype(jnp.float32)
        y = stage_one([x[:, s * LANES:(s + 1) * LANES] for s in range(16)])
        for s in range(SLICES):
            both = jnp.concatenate(y[s], axis=1)
            top = both.astype(jnp.bfloat16)
            first[s, start:start + 16, :] = top
            second[s, start:start + 16, :] = (both - top.astype(jnp.float32)).astype(jnp.bfloat16)
    spectra = []
    power = jnp.zeros((rows, LANES), jnp.float32)
    for s in range(SLICES):
        z = jnp.dot(first[s], table[s], preferred_element_type=jnp.float32)
        z += jnp.dot(second[s], table[s], preferred_element_type=jnp.float32)
        spectra.append(z)
        power += z[:, :LANES] * z[:, :LANES] + z[:, LANES:] * z[:, LANES:]
    row = lax.broadcasted_iota(jnp.int32, (LANES, LANES), 0) % (LANES // 2) // (WBLK // 16)
    column = lax.broadcasted_iota(jnp.int32, (LANES, LANES), 1) % (LANES // 2) // (WBLK // 16)
    band = jnp.where(row == column, 1.0, 0.0)
    bands = jnp.dot(power, band, precision=lax.Precision.HIGHEST, preferred_element_type=jnp.float32)
    factor = lax.rsqrt(bands * (1.0 / WBLK) + 1e-05)
    keep = jnp.concatenate(
        [jnp.broadcast_to(flags[:, w:w + 1], (stations, LANES)) for w in range(windows)], axis=0
    )
    corner = lax.broadcasted_iota(jnp.int32, (rows, LANES), 1) == 0
    to = lax.broadcasted_iota(jnp.int32, (rows, rows), 0)
    source = lax.broadcasted_iota(jnp.int32, (rows, rows), 1)
    moved = (to // stations == source % windows) & (to % stations == source // windows)
    moved = jnp.where(moved, 1.0, 0.0).astype(jnp.bfloat16)
    factor = jnp.concatenate([factor, factor], axis=1)
    keep = jnp.concatenate([keep, keep], axis=1)
    for s in range(SLICES):
        white = (spectra[s] * factor).astype(jnp.bfloat16)
        white = jnp.dot(moved, white, preferred_element_type=jnp.float32) * keep
        real, imag = white[:, :LANES], white[:, LANES:]
        if s == 0:
            imag = jnp.where(corner, keep[:, :LANES], imag)
        out[:, s * LANES:(s + 1) * LANES] = real.astype(jnp.bfloat16)
        out[:, F + s * LANES:F + (s + 1) * LANES] = imag.astype(jnp.bfloat16)


def forward(traces, gaps):
    stations, windows, samples = traces.shape
    rows = stations * windows
    signs = jnp.sign(traces.reshape(rows, samples)).astype(jnp.bfloat16)
    table = jnp.asarray(forward_table()) * lax.optimization_barrier(jnp.ones((), jnp.bfloat16))
    return pl.pallas_call(
        functools.partial(forward_kernel, stations, windows),
        out_shape=jax.ShapeDtypeStruct((rows, 2 * F), jnp.bfloat16),
        scratch_shapes=[
            pltpu.VMEM((SLICES, rows, 2 * LANES), jnp.bfloat16),
            pltpu.VMEM((SLICES, rows, 2 * LANES), jnp.bfloat16),
        ],
        compiler_params=pltpu.CompilerParams(vmem_limit_bytes=16 * 1024 * 1024),
        cost_estimate=pl.CostEstimate(flops=6 * rows * F * 512, bytes_accessed=4 << 20, transcendentals=rows * LANES),
        name="whiten",
    )(signs, gaps.astype(jnp.float32), table)


def unit_kernel(stations, windows, parts, choose, *refs):
    x_ref, refs = refs[0], refs[1:]
    y_refs, refs = refs[:2 if choose else 1], refs[2 if choose else 1:]
    table, edge = refs[:2]
    outs = refs[2:2 + parts]
    xf, yf, x0, y0, cross, fold, total, edges, counts = refs[2 + parts:]
    pairs = stations * stations
    rows = stations * windows
    me = lax.axis_index("win")

    def load(source, target, corner):
        lane = lax.broadcasted_iota(jnp.int32, (rows, LANES), 1) == 0
        for s in range(2 * SLICES):
            at = slice(s * LANES, (s + 1) * LANES)
            value = source[:, at].astype(jnp.float32)
            if s == SLICES:
                corner[...] = value.reshape(corner.shape)
                value = jnp.where(lane, 0.0, value)
            target[:, :, at] = value.reshape(windows, stations, LANES)

    load(x_ref, xf, x0)
    if choose:
        odd = lax.rem(lax.axis_index("sta"), 2)

        @pl.when(odd == 0)
        def _():
            load(y_refs[0], yf, y0)

        @pl.when(odd == 1)
        def _():
            load(y_refs[1], yf, y0)
    else:
        load(y_refs[0], yf, y0)

    total[...] = jnp.zeros_like(total)
    edges[...] = jnp.zeros_like(edges)
    counts[...] = jnp.zeros_like(counts)

    def step(chunk, carry):
        for v in range(STACK):
            w = chunk * STACK + v
            for i in range(0, stations, 2):
                folded = [[], [], [], []]
                for e in range(2):
                    at = pl.ds((i + e) * stations, stations)
                    counts[at, :] += x0[w, i + e:i + e + 1, :] * y0[w]
                spot = pl.ds(v * pairs + i * stations, 2 * stations)
                reals, imags = [], []
                for s in range(SLICES):
                    re = slice(s * LANES, (s + 1) * LANES)
                    im = slice(F + s * LANES, F + (s + 1) * LANES)
                    yr, yi = yf[w, :, re], yf[w, :, im]
                    halves = []
                    for e in range(2):
                        xr, xi = xf[w, i + e:i + e + 1, re], xf[w, i + e:i + e + 1, im]
                        halves.append((xr * yr + xi * yi, xi * yr - xr * yi))
                    cr = jnp.concatenate([h[0] for h in halves], axis=0)
                    ci = jnp.concatenate([h[1] for h in halves], axis=0)
                    reals.append(cr)
                    imags.append(ci)
                    cross[0, spot, re] = cr.astype(jnp.bfloat16)
                    cross[1, spot, re] = ci.astype(jnp.bfloat16)
                for k, c in enumerate((reals, imags)):
                    cosine = (c[0] - c[4]) + ROOT * ((c[1] + c[7]) - (c[3] + c[5]))
                    sine = (c[2] - c[6]) + ROOT * ((c[1] + c[3]) - (c[5] + c[7]))
                    fold[spot, 2 * k * LANES:(2 * k + 1) * LANES] = cosine.astype(jnp.bfloat16)
                    fold[spot, (2 * k + 1) * LANES:(2 * k + 2) * LANES] = sine.astype(jnp.bfloat16)
        from_real = jnp.dot(cross[0], table[...], preferred_element_type=jnp.float32)
        from_imag = jnp.dot(cross[1], table[...], preferred_element_type=jnp.float32)
        rim = jnp.dot(fold[...], edge[...], preferred_element_type=jnp.float32)
        sums = [None] * 9
        for v in range(STACK):
            at = slice(v * pairs, (v + 1) * pairs)
            p, r = from_real[at, :HALF], from_real[at, HALF:]
            s, q = from_imag[at, :HALF], from_imag[at, HALF:]
            terms = []
            for real, imag in ((p - q, r + s), (p + q, s - r), (rim[at, :LANES], rim[at, LANES:])):
                scale = lax.rsqrt(jnp.maximum(real * real + imag * imag, 0.25))
                terms += [real, real * scale, imag * scale]
            sums = terms if v == 0 else [a + b for a, b in zip(sums, terms)]
        for k in range(6):
            total[k] += sums[k]
        for k in range(3):
            edges[k] += sums[6 + k]
        return carry

    lax.fori_loop(0, windows // STACK, step, 0)

    scales = (32766.0 / (PEAK * windows), 32000.0 / windows, 32000.0 / windows)
    wide = LAGS // parts

    def piece(z):
        if z < parts // 2:
            return 1, (parts // 2 - 1 - z) * wide
        return 0, (z - parts // 2) * wide

    lane = lax.broadcasted_iota(jnp.int32, (pairs, LANES), 1)
    last = jnp.zeros((pairs, LANES), jnp.float32)
    for z in range(parts):
        side, start = piece(z)
        for k in range(3):
            if start + wide < HALF:
                column = total[3 * side + k, :, start + wide:start + wide + 1]
            else:
                column = edges[k, :, side:side + 1]
            last = jnp.where(lane == 4 * z + k, column * scales[k], last)
        last = jnp.where(lane == 4 * z + 3, counts[:, 0:1], last)
    turned = jnp.transpose(last)

    def whole(value):
        return jnp.round(value).astype(jnp.int32).astype(jnp.int16)

    for here in range(parts):
        @pl.when(me == here)
        def _():
            for d in range(parts):
                z = here ^ d
                side, start = piece(z)
                for k in range(3):
                    part = total[3 * side + k, :, start:start + wide] * scales[k]
                    outs[d][k * pairs:(k + 1) * pairs, 0:wide] = whole(part)
                tail = turned[4 * z:4 * z + 4]
                tail = jnp.concatenate([tail, jnp.zeros((EXTRA - 4, pairs), jnp.float32)], axis=0)
                outs[d][3 * pairs:3 * pairs + EXTRA, 0:pairs] = whole(tail)


def unit(stations, parts, own, others, name):
    rows = own.shape[0]
    windows = rows // stations
    pairs = stations * stations
    choose = len(others) == 2
    shape = jax.ShapeDtypeStruct((3 * pairs + EXTRA, LANES), jnp.int16)
    return pl.pallas_call(
        functools.partial(unit_kernel, stations, windows, parts, choose),
        out_shape=[shape] * parts,
        scratch_shapes=[
            pltpu.VMEM((windows, stations, 2 * F), jnp.float32),
            pltpu.VMEM((windows, stations, 2 * F), jnp.float32),
            pltpu.VMEM((windows, stations, LANES), jnp.float32),
            pltpu.VMEM((windows, stations, LANES), jnp.float32),
            pltpu.VMEM((2, STACK * pairs, F), jnp.bfloat16),
            pltpu.VMEM((STACK * pairs, 4 * LANES), jnp.bfloat16),
            pltpu.VMEM((6, pairs, HALF), jnp.float32),
            pltpu.VMEM((3, pairs, LANES), jnp.float32),
            pltpu.VMEM((pairs, LANES), jnp.float32),
        ],
        compiler_params=pltpu.CompilerParams(vmem_limit_bytes=24 * 1024 * 1024),
        cost_estimate=pl.CostEstimate(
            flops=4 * rows * stations * F * LAGS, bytes_accessed=3 << 20, transcendentals=rows * stations * LAGS
        ),
        name=name,
    )(own, *others, jnp.asarray(inverse_table()), jnp.asarray(edge_table()))


def finish_kernel(stations, windows, parts, back, *refs):
    sums = refs[:parts]
    outs = refs[parts:]
    pairs = stations * stations
    wide = LAGS // parts
    negative = lax.axis_index("win") < parts // 2
    everything = sums[0][...].astype(jnp.int32).astype(jnp.float32)
    for ref in sums[1:]:
        everything = everything + ref[...].astype(jnp.int32).astype(jnp.float32)
    scales = (PEAK * windows / 32766.0, windows / 32000.0, windows / 32000.0)
    row = lax.broadcasted_iota(jnp.int32, (LANES, LANES), 0)
    column = lax.broadcasted_iota(jnp.int32, (LANES, LANES), 1)
    mirror = jnp.where((row + column == wide) & (column > 0) & (column < wide), 1.0, 0.0)
    lane = lax.broadcasted_iota(jnp.int32, (pairs, LANES), 1)
    row = lax.broadcasted_iota(jnp.int32, (pairs, pairs), 0)
    column = lax.broadcasted_iota(jnp.int32, (pairs, pairs), 1)
    swap = (row // stations == column % stations) & (row % stations == column // stations)
    swap = jnp.where(swap, 1.0, 0.0)
    if True:
        acc = everything
        tail = jnp.transpose(acc[3 * pairs:])[:pairs]
        inverse = 1.0 / jnp.maximum(tail[:, 3:4], 1.0)

        def stack(linear, real, imag):
            linear = linear * scales[0] * inverse
            real = real * scales[1] * inverse
            imag = imag * scales[2] * inverse
            return linear * (real * real + imag * imag)

        plain = stack(acc[:pairs], acc[pairs:2 * pairs], acc[2 * pairs:3 * pairs])
        edge = stack(tail[:, 0:1], tail[:, 1:2], tail[:, 2:3])
        turned = jnp.dot(plain, mirror, precision=lax.Precision.HIGHEST, preferred_element_type=jnp.float32)
        turned = jnp.where(lane == 0, edge, turned)
        outs[0][...] = jnp.where(negative, turned, plain)
        if back:
            value = jnp.where(negative, plain, turned)
            outs[1][...] = jnp.dot(
                swap, value, precision=lax.Precision.HIGHEST, preferred_element_type=jnp.float32
            )


def finish(stations, windows, sums, back, name):
    pairs = stations * stations
    parts = len(sums)
    shape = jax.ShapeDtypeStruct((pairs, LANES), jnp.float32)
    return pl.pallas_call(
        functools.partial(finish_kernel, stations, windows, parts, back),
        out_shape=[shape] * (2 if back else 1),
        compiler_params=pltpu.CompilerParams(vmem_limit_bytes=16 * 1024 * 1024),
        cost_estimate=pl.CostEstimate(flops=1 << 22, bytes_accessed=1 << 18, transcendentals=0),
        name=name,
    )(*sums)


def exchange(sums):
    parts = len(sums)
    return [sums[0]] + [
        lax.ppermute(sums[d], "win", [(i, i ^ d) for i in range(parts)]) for d in range(parts - 1, 0, -1)
    ]


def local(traces, gap_mask, pair_mask):
    blocks = lax.axis_size("sta")
    parts = lax.axis_size("win")
    stations, windows, _ = traces.shape
    white = forward(traces, gap_mask)
    second = lax.ppermute(white, "sta", [((i + 2) % blocks, i) for i in range(blocks)])
    beside = lax.ppermute(white, "sta", [(i ^ 1, i) for i in range(blocks)])
    own_sums = exchange(unit(stations, parts, white, [white], "stack0"))
    second, *own_sums = lax.optimization_barrier((second, *own_sums))
    handed = lax.ppermute(second, "sta", [(i ^ 1, i) for i in range(blocks)])
    far_sums = exchange(unit(stations, parts, white, [second], "stack2"))
    near_sums = exchange(unit(stations, parts, white, [beside, handed], "stack1"))

    def returned(value, distance):
        route = []
        for b in range(blocks):
            for z in range(parts):
                route.append((b * parts + z, ((b + distance) % blocks) * parts + parts - 1 - z))
        return lax.ppermute(value, ("sta", "win"), route)

    far, far_back = finish(stations, windows, far_sums, True, "finish2")
    far_back = returned(far_back, 2)
    (middle,) = finish(stations, windows, own_sums, False, "finish0")
    near, near_back = finish(stations, windows, near_sums, True, "finish1")
    near_back = returned(near_back, 1)
    wide = LAGS // parts
    pws = jnp.stack(
        [value.reshape(stations, stations, LANES)[..., :wide] for value in (far_back, near_back, middle, near, far)], axis=1
    )
    return pws * pair_mask.astype(jnp.float32)[..., None]


def solution(mesh):
    return jax.shard_map(
        local,
        mesh=mesh,
        in_specs=(P("sta", "win", None), P("sta", "win"), P("sta", None, None)),
        out_specs=P("sta", None, None, "win"),
        check_vma=False,
    )
```
